256 devices in a mesh: aux: 32 (over x, y, z_lo), grp: 8 (over z_hi, core).
Axes of the slice: x: 4, y: 4, z: 8 (z_hi: 4, z_lo: 2; z = z_hi * 2 + z_lo), core: 2. Of those that a mesh axis runs over, the one named last changes fastest.
Arguments:
- integrals: bfloat16 [8192, 16, 4096], P(('aux', 'grp')), may hold values from -6 to 6
- block_pairs: int32 [256, 16, 2], P(('aux', 'grp')), may hold values from 0 to 63
- occupied: bfloat16 [2, 4096], replicated, may hold values from -0.75 to 0.75
- virtual: bfloat16 [4096, 3072], P(None, 'grp'), may hold values from -0.1875 to 0.1875
- stored: bfloat16 [8192, 6144], P('aux'), may hold values from -0.0625 to 0.0625
Outputs:
- exchange_panel: bfloat16 [2, 3072, 2, 3072], P(None, ('grp', 'aux'))
The draws below stay inside these ranges and needn't reach their ends.
Inputs may be any that keep to these rules, and one draw needn't show every extreme that they name: `block_pairs`: block pairs may repeat within a shard; repeated blocks add.
All inputs are finite; a program needn't handle non-finite values.
Results may differ from the reference program's by a relative error of at most 0.0095.
Values may be sent and summed in bfloat16 or wider, within the bound.
No kernel may reach another device: no remote copies, remote signals or barrier semaphores. Data moves between devices by JAX's collectives and lax.ppermute only.
A program may use at most 128 MiB of HBM per device.

```python
import jax
import jax.numpy as jnp
from jax import lax

NBAS = 4096
BLK = 64
V = 3072
NOCC = 2
JWIN = 2
AUX_DEV = 32
NB = 16
SHARDS = 256
NAUX = 8192
N_AUX = 32
N_GRP = 8


def place_ends(entries, key, low, largest):
    index_at = [jax.random.randint(jax.random.fold_in(key, axis), (), 0, length) for axis, length in enumerate(entries.shape)]
    widest = entries.shape.index(max(entries.shape))
    neighbour = index_at[:widest] + [(index_at[widest] + 1) % entries.shape[widest]] + index_at[widest + 1:]
    return entries.at[tuple(index_at)].set(low).at[tuple(neighbour)].set(largest)


def block_scale(rng, shape, split, least, high):
    loudness = 1.0
    for dim, blocks in split:
        heights = jax.random.uniform(jax.random.fold_in(jax.random.fold_in(rng, 6), dim), (blocks,), jnp.float32, least / len(split), high / len(split))
        loudness = loudness * jnp.repeat(jnp.exp(heights), shape[dim] // blocks).reshape((-1,) + (1,) * (len(shape) - 1 - dim))
    return loudness


def centred(rng, dims, spread, bound, pieces=(), held_as=jnp.bfloat16):
    values = jax.random.normal(rng, dims, jnp.float32) * spread
    if len(pieces) > 0:
        values = block_scale(rng, dims, pieces, -0.22, 0.18) * values
    return jnp.clip(values, min=-bound, max=bound).astype(held_as)


def setup_inputs(seed: int = 0) -> dict:
    splits = jax.random.split(jax.random.key(seed), 6)
    integrals = centred(splits[0], (NAUX, NB, BLK * BLK), 1.0, 6.0, ((0, 256),))
    block_pairs = place_ends(jax.random.randint(splits[1], (SHARDS, NB, 2), 0, NBAS // BLK), jax.random.fold_in(splits[1], 1), 0, (NBAS // BLK) - 1).astype(jnp.int32)
    occupied = centred(splits[2], (NOCC, NBAS), BLK ** -0.5, 0.75)
    virtual = centred(splits[3], (NBAS, V), (BLK * NB) ** -0.5, 0.1875, ((1, 8),))
    stored = centred(splits[4], (NAUX, JWIN * V), NAUX ** -0.5, 0.0625, ((0, 32),))
    return dict(integrals=integrals, block_pairs=block_pairs, occupied=occupied, virtual=virtual, stored=stored)


def shard_factor(tiles, pairs, occupied, virtual):
    nblocks = NBAS // BLK
    block_iota = jnp.arange(nblocks, dtype=jnp.int32)
    row_pick = (pairs[:, 0:1] == block_iota[None, :]).astype(jnp.float32)
    col_pick = (pairs[:, 1:2] == block_iota[None, :]).astype(jnp.float32)
    occ_blocks = occupied.astype(jnp.float32).reshape(NOCC, nblocks, BLK)
    picked = jnp.einsum('ikm,bk->ibm', occ_blocks, row_pick)
    squares = tiles.astype(jnp.float32).reshape(AUX_DEV, NB, BLK, BLK)
    partial_value = jnp.einsum('ibm,pbmn->pibn', picked, squares)
    half = jnp.einsum('pibn,bk->pikn', partial_value, col_pick).reshape(AUX_DEV * NOCC, NBAS).astype(jnp.bfloat16)
    factor = jnp.dot(half, virtual, preferred_element_type=jnp.float32).astype(jnp.bfloat16)
    return factor.reshape(AUX_DEV, NOCC, V).transpose(0, 2, 1).reshape(AUX_DEV, V * NOCC)


def reference(integrals, block_pairs, occupied, virtual, stored):
    shard_count = N_AUX * N_GRP
    tiles_all = integrals.reshape(shard_count, AUX_DEV, NB, BLK * BLK)
    stored_all = stored.reshape(shard_count, AUX_DEV, JWIN * V)

    def step(carry, inputs):
        tiles, pairs, rows = inputs
        factor = shard_factor(tiles, pairs, occupied, virtual)
        term = lax.dot_general(factor, rows, (((0,), (0,)), ((), ())), preferred_element_type=jnp.float32)
        return carry + term, None

    start = jnp.zeros((V * NOCC, JWIN * V), jnp.float32)
    total, unused = lax.scan(step, start, (tiles_all, block_pairs, stored_all))
    result = total.astype(jnp.bfloat16).reshape(V, NOCC, JWIN, V)
    return result.transpose(1, 0, 2, 3)
```

```python
import functools

import jax
import jax.numpy as jnp
from jax import lax
from jax.experimental import pallas as pl
from jax.experimental.pallas import tpu as pltpu
from jax.sharding import PartitionSpec as P

NBAS = 4096
BLK = 64
V = 3072
NOCC = 2
JWIN = 2
NB = 16
PDEV = 32
RING = 4
SLAB = 384
NCOL = 1536
HCOL = 768
ROWS = 24
NCOMP = NB * BLK

F32 = jnp.float32
BF16 = jnp.bfloat16
VMEM = pl.BlockSpec(memory_space=pltpu.VMEM)
SMEM = pl.BlockSpec(memory_space=pltpu.SMEM)


def params():
    return pltpu.CompilerParams(vmem_limit_bytes=40 * 1024 * 1024)


def shift_x(d):
    return [(a, ((a // 8 + d) % 4) * 8 + a % 8) for a in range(32)]


def shift_y(d):
    return [(a, (a // 8) * 8 + ((a // 2 + d) % 4) * 2 + a % 2) for a in range(32)]


SWAP_ZL = [(a, a ^ 1) for a in range(32)]
SWAP_CORE = [(g, g ^ 1) for g in range(8)]


def shift_zh(d):
    return [(g, (g + 2 * d) % 8) for g in range(8)]


P_STEP = 8


def half_kernel(mu_ref, occ_ref, x_ref, o_ref, w_ref):
    step = pl.program_id(0)

    @pl.when(step == 0)
    def _():
        pick = (mu_ref[...] == lax.broadcasted_iota(jnp.int32, (NB, BLK), 1)).astype(BF16)
        lane = lax.broadcasted_iota(jnp.int32, (BLK, BLK * BLK), 1)
        row = lax.broadcasted_iota(jnp.int32, (BLK, BLK * BLK), 0)
        spread = (lane // BLK == row).astype(BF16)
        for i in range(NOCC):
            rows = jnp.dot(pick, occ_ref[i], preferred_element_type=F32).astype(BF16)
            w_ref[i] = jnp.dot(rows, spread, preferred_element_type=F32)

    acc = [[jnp.zeros((NB, 128), F32) for _ in range(NOCC)] for _ in range(P_STEP)]
    for t in range(BLK * BLK // 128):
        cols = slice(t * 128, (t + 1) * 128)
        w = [w_ref[i, :, cols] for i in range(NOCC)]
        for p in range(P_STEP):
            x = x_ref[p, :, cols].astype(F32)
            for i in range(NOCC):
                acc[p][i] = acc[p][i] + x * w[i]
    rows = P_STEP * NB
    lane = lax.broadcasted_iota(jnp.int32, (rows, NCOMP), 1)
    row = lax.broadcasted_iota(jnp.int32, (rows, NCOMP), 0)
    mine = lane // BLK == row % NB
    srow = lax.broadcasted_iota(jnp.int32, (P_STEP, rows), 0)
    scol = lax.broadcasted_iota(jnp.int32, (P_STEP, rows), 1)
    collect = (scol // NB == srow).astype(BF16)
    for i in range(NOCC):
        a = jnp.concatenate([acc[p][i] for p in range(P_STEP)], axis=0)
        both = a + pltpu.roll(a, BLK, 1)
        wide = jnp.concatenate([both] * (NCOMP // 128), axis=1)
        placed = jnp.where(mine, wide, 0.0).astype(BF16)
        o_ref[i, 0] = jnp.dot(collect, placed, preferred_element_type=F32)


def half_transform(integrals, pairs, occupied):
    mu = pairs[:, 0:1]
    occ = occupied.reshape(NOCC, NBAS // BLK, BLK)
    out = pl.pallas_call(
        half_kernel,
        grid=(PDEV // P_STEP,),
        in_specs=[
            pl.BlockSpec((NB, 1), lambda s: (0, 0)),
            pl.BlockSpec((NOCC, NBAS // BLK, BLK), lambda s: (0, 0, 0)),
            pl.BlockSpec((P_STEP, NB, BLK * BLK), lambda s: (s, 0, 0)),
        ],
        out_specs=pl.BlockSpec((NOCC, 1, P_STEP, NCOMP), lambda s: (0, s, 0, 0)),
        out_shape=jax.ShapeDtypeStruct((NOCC, PDEV // P_STEP, P_STEP, NCOMP), F32),
        scratch_shapes=[pltpu.VMEM((NOCC, NB, BLK * BLK), F32)],
        compiler_params=params(),
        name="half",
    )(mu, occ, integrals)
    return out.reshape(NOCC * PDEV, NCOMP).astype(BF16)


def factor_kernel(pos_ref, nu_ref, *refs):
    halves = refs[:8]
    v_ref, f0_ref, f1_ref, pick_ref = refs[8:]
    zh, core = pos_ref[3], pos_ref[4]
    for s in range(8):
        d, other = s // 2, s % 2
        c = 1 - core if other else core
        g = lax.rem(zh - d + 4, 4) * 2 + c
        slot = s % 2
        for k in range(NB):
            n = nu_ref[g * NB + k]
            pick_ref[slot, k * BLK : (k + 1) * BLK, :] = v_ref[pl.ds(pl.multiple_of(n * BLK, BLK), BLK), :]
        f = jnp.dot(halves[s][...], pick_ref[slot], preferred_element_type=F32).astype(BF16)
        rows = pl.ds(pl.multiple_of(g * PDEV, PDEV), PDEV)
        f0_ref[rows, :] = f[:PDEV]
        f1_ref[rows, :] = f[PDEV:]


def factors(pos, nu, halves, virtual):
    out = jax.ShapeDtypeStruct((8 * PDEV, SLAB), BF16)
    return pl.pallas_call(
        factor_kernel,
        in_specs=[SMEM, SMEM] + [VMEM] * 9,
        out_specs=[VMEM, VMEM],
        out_shape=[out, out],
        scratch_shapes=[pltpu.VMEM((2, NCOMP, SLAB), BF16)],
        compiler_params=params(),
        name="factor",
    )(pos, nu, *halves, virtual)


def panel_kernel(swap, pos_ref, *refs):
    f = refs[0:4]
    mine = refs[4:8]
    other = refs[8:12]
    outs = refs[12:16]
    acc_ref = refs[16]
    dims = (((0,), (0,)), ((), ()))
    for h, part in enumerate((mine, other)):
        total = None
        for d in range(4):
            term = lax.dot_general(f[d][...], part[d][...], dims, preferred_element_type=F32)
            total = term if total is None else total + term
        acc_ref[:, h * HCOL : (h + 1) * HCOL] = total
    me = pos_ref[0] if swap else pos_ref[1]
    for d in range(4):
        to = lax.rem(me + d, 4)
        for k in range(4):
            start = to * 96 + k * ROWS if swap else k * 96 + to * ROWS
            outs[d][k] = acc_ref[pl.ds(pl.multiple_of(start, 8), ROWS), :].astype(BF16)


def panel(swap, pos, f, mine, other, stored):
    def own(flip):
        def index(s, pos_ref):
            at = pos_ref[1] if swap else pos_ref[0]
            c = 1 - pos_ref[4] if flip else pos_ref[4]
            return (0, at * 2 + c)

        return pl.BlockSpec((256, HCOL), index)

    fspec = pl.BlockSpec((256, SLAB), lambda s, pos_ref: (0, 0))
    sspec = pl.BlockSpec((256, HCOL), lambda s, pos_ref: (0, 0))
    ospec = pl.BlockSpec((4, ROWS, NCOL), lambda s, pos_ref: (0, 0, 0))
    out = jax.ShapeDtypeStruct((4, ROWS, NCOL), BF16)
    return pl.pallas_call(
        functools.partial(panel_kernel, swap),
        grid_spec=pltpu.PrefetchScalarGridSpec(
            num_scalar_prefetch=1,
            grid=(1,),
            in_specs=[fspec] * 4 + [own(False)] + [sspec] * 3 + [own(True)] + [sspec] * 3,
            out_specs=[ospec] * 4,
            scratch_shapes=[pltpu.VMEM((SLAB, NCOL), F32)],
        ),
        out_shape=[out] * 4,
        compiler_params=params(),
        name="panel_b" if swap else "panel_a",
    )(pos, *f, stored, *mine, stored, *other)


def sum_kernel(pos_ref, *refs):
    keep_ref, send_ref = refs[8:]
    low = pos_ref[2] == 0
    for r in range(2):
        parts = refs[4 * r : 4 * r + 4]
        for k in range(4):
            total = parts[0][k].astype(F32)
            for d in range(1, 4):
                total = total + parts[d][k].astype(F32)
            lo, hi = total[:12], total[12:]
            keep_ref[r, k] = jnp.where(low, lo, hi)
            send_ref[r, k] = jnp.where(low, hi, lo).astype(BF16)


def ring_sum(pos, a, b):
    return pl.pallas_call(
        sum_kernel,
        in_specs=[SMEM] + [VMEM] * 8,
        out_specs=[VMEM, VMEM],
        out_shape=[
            jax.ShapeDtypeStruct((2, 4, 12, NCOL), F32),
            jax.ShapeDtypeStruct((2, 4, 12, NCOL), BF16),
        ],
        compiler_params=params(),
        name="ring_sum",
    )(pos, *a, *b)


def pair_kernel(pos_ref, keep_ref, got_ref, *outs):
    for r in range(2):
        me = pos_ref[r]
        for d in range(4):
            k = lax.rem(me + d, 4)
            outs[4 * r + d][...] = (keep_ref[r, k] + got_ref[r, k].astype(F32)).astype(BF16)


def pair_sum(pos, keep, got):
    return pl.pallas_call(
        pair_kernel,
        in_specs=[SMEM, VMEM, VMEM],
        out_specs=[VMEM] * 8,
        out_shape=[jax.ShapeDtypeStruct((12, NCOL), BF16)] * 8,
        compiler_params=params(),
        name="pair_sum",
    )(pos, keep, got)


def place_kernel(pos_ref, *refs):
    o_ref = refs[8]
    core = pos_ref[4]
    for r in range(2):
        for d in range(4):
            at = lax.rem(pos_ref[r] - d + 4, 4) * NCOL
            block = refs[4 * r + d]
            for h in range(2):
                half = 1 - core if h else core
                cols = pl.ds(pl.multiple_of(at + half * HCOL, 128), HCOL)
                o_ref[r, :, cols] = block[:, h * HCOL : (h + 1) * HCOL]


def place(pos, a, b):
    return pl.pallas_call(
        place_kernel,
        in_specs=[SMEM] + [VMEM] * 8,
        out_specs=VMEM,
        out_shape=jax.ShapeDtypeStruct((2, 12, JWIN * V), BF16),
        compiler_params=params(),
        name="place",
    )(pos, *a, *b)


def per_device(integrals, block_pairs, occupied, virtual, stored):
    aux, grp = lax.axis_index("aux"), lax.axis_index("grp")
    x, y, zl = aux // 8, (aux // 2) % 4, aux % 2
    zh, core = grp // 2, grp % 2
    pos = jnp.stack([x, y, zl, zh, core]).astype(jnp.int32)
    order = (1, 3, 2)

    def column(at):
        return lax.dynamic_slice(stored, (0, (at * 2 + core) * HCOL), (256, HCOL))

    got_a, got_b = {}, {}
    for d in order:
        got_a[d] = lax.ppermute(column((x + d) % 4), "aux", shift_x(d))
        got_b[d] = lax.ppermute(column((y + d) % 4), "aux", shift_y(d))
    nu = lax.all_gather(block_pairs[0, :, 1], "grp", axis=0, tiled=True)

    half = half_transform(integrals, block_pairs[0], occupied)
    halves = {0: half}
    for d in order:
        halves[d] = lax.ppermute(half, "grp", shift_zh(d))
    pieces = []
    for d in range(4):
        pieces += [halves[d], lax.ppermute(halves[d], "grp", SWAP_CORE)]
    oth_a = {d: lax.ppermute(got_a[d], "grp", SWAP_CORE) for d in order}
    oth_b = {d: lax.ppermute(got_b[d], "grp", SWAP_CORE) for d in order}

    f0, f1 = factors(pos, nu, pieces, virtual)
    fa, fb = {0: f0}, {0: f1}
    for d in order:
        fa[d] = lax.ppermute(f0, "aux", shift_x(d))
        fb[d] = lax.ppermute(f1, "aux", shift_y(d))
    ring = range(4)
    pa = panel(False, pos, [fa[d] for d in ring], [got_a[d] for d in (1, 2, 3)], [oth_a[d] for d in (1, 2, 3)], stored)
    pb = panel(True, pos, [fb[d] for d in ring], [got_b[d] for d in (1, 2, 3)], [oth_b[d] for d in (1, 2, 3)], stored)
    ra, rb = {0: pa[0]}, {0: pb[0]}
    for d in order:
        ra[d] = lax.ppermute(pa[d], "aux", shift_y(d))
        rb[d] = lax.ppermute(pb[d], "aux", shift_x(d))
    keep, send = ring_sum(pos, [ra[d] for d in ring], [rb[d] for d in ring])
    got = lax.ppermute(send, "aux", SWAP_ZL)
    ends = pair_sum(pos, keep, got)
    ea, eb = {0: ends[0]}, {0: ends[4]}
    for d in order:
        ea[d] = lax.ppermute(ends[d], "aux", shift_x(d))
        eb[d] = lax.ppermute(ends[4 + d], "aux", shift_y(d))
    out = place(pos, [ea[d] for d in ring], [eb[d] for d in ring])
    return out.reshape(NOCC, 12, JWIN, V)


def solution(mesh):
    in_specs = (
        P(("aux", "grp"), None, None),
        P(("aux", "grp"), None, None),
        P(),
        P(None, "grp"),
        P("aux", None),
    )
    out_specs = P(None, ("grp", "aux"), None, None)
    return jax.shard_map(
        per_device, mesh=mesh, in_specs=in_specs, out_specs=out_specs, check_vma=False
    )
```

```python
import functools

import jax
import jax.numpy as jnp
from jax import lax
from jax.experimental import pallas as pl
from jax.experimental.pallas import tpu as pltpu
from jax.sharding import PartitionSpec as P

NBAS = 4096
BLK = 64
V = 3072
NOCC = 2
JWIN = 2
NB = 16
PDEV = 32
RING = 4
SLAB = 384
NCOL = 1536
HCOL = 768
ROWS = 24
NCOMP = NB * BLK
KDIM = 8 * PDEV

F32 = jnp.float32
BF16 = jnp.bfloat16
VMEM = pl.BlockSpec(memory_space=pltpu.VMEM)
SMEM = pl.BlockSpec(memory_space=pltpu.SMEM)


def params(mib):
    return pltpu.CompilerParams(vmem_limit_bytes=mib * 1024 * 1024)


CHEAP = pl.CostEstimate(flops=0, bytes_accessed=0, transcendentals=0)


def shift_x(d):
    return [(a, ((a // 8 + d) % 4) * 8 + a % 8) for a in range(32)]


SWAP_CORE = [(g, g ^ 1) for g in range(8)]


def shift_zh(d):
    return [(g, (g + 2 * d) % 8) for g in range(8)]


P_STEP = 8
WIDE = NCOMP + 128


LOADS = 4


def half_kernel(pairs_ref, occ_ref, *refs):
    xs = refs[:LOADS]
    o_ref, w_ref, sum_ref = refs[LOADS:]
    step = pl.program_id(0)

    @pl.when(step == 0)
    def _():
        pick = (pairs_ref[:, 0:1] == lax.broadcasted_iota(jnp.int32, (NB, BLK), 1)).astype(BF16)
        lane = lax.broadcasted_iota(jnp.int32, (BLK, BLK * BLK), 1)
        row = lax.broadcasted_iota(jnp.int32, (BLK, BLK * BLK), 0)
        spread = (lane // BLK == row).astype(BF16)
        for i in range(NOCC):
            rows = jnp.dot(pick, occ_ref[i], preferred_element_type=F32).astype(BF16)
            w_ref[i] = jnp.dot(rows, spread, preferred_element_type=F32)

    acc = [[jnp.zeros((NB, 128), F32) for _ in range(NOCC)] for _ in range(P_STEP)]
    for t in range(BLK * BLK // 128):
        cols = slice(t * 128, (t + 1) * 128)
        w = [w_ref[i, :, cols] for i in range(NOCC)]
        for p in range(P_STEP):
            x = xs[p * LOADS // P_STEP][p % (P_STEP // LOADS), :, cols].astype(F32)
            for i in range(NOCC):
                acc[p][i] = acc[p][i] + x * w[i]
    rows = P_STEP * NB
    lane = lax.broadcasted_iota(jnp.int32, (rows, NCOMP), 1)
    row = lax.broadcasted_iota(jnp.int32, (rows, NCOMP), 0)
    mine = lane // BLK == row % NB
    srow = lax.broadcasted_iota(jnp.int32, (P_STEP, rows), 0)
    scol = lax.broadcasted_iota(jnp.int32, (P_STEP, rows), 1)
    collect = (scol // NB == srow).astype(BF16)
    for i in range(NOCC):
        a = jnp.concatenate([acc[p][i] for p in range(P_STEP)], axis=0)
        both = a + pltpu.roll(a, BLK, 1)
        wide = jnp.concatenate([both] * (NCOMP // 128), axis=1)
        placed = jnp.where(mine, wide, 0.0).astype(BF16)
        at = pl.ds(pl.multiple_of(step * P_STEP, P_STEP), P_STEP)
        sum_ref[i, at, :] = jnp.dot(collect, placed, preferred_element_type=F32)

    @pl.when(step == PDEV // P_STEP - 1)
    def _():
        nrow = lax.broadcasted_iota(jnp.int32, (NB, 128), 0)
        ncol = lax.broadcasted_iota(jnp.int32, (NB, 128), 1)
        named = jnp.sum(jnp.where(nrow == ncol, pairs_ref[:, 1:2].astype(F32), 0.0), axis=0, keepdims=True)
        for i in range(NOCC):
            o_ref[i * PDEV : (i + 1) * PDEV, :NCOMP] = sum_ref[i].astype(BF16)
            o_ref[i * PDEV : (i + 1) * PDEV, NCOMP:] = jnp.broadcast_to(named, (PDEV, 128)).astype(BF16)


def half_transform(integrals, pairs, occupied):
    occ = occupied.reshape(NOCC, NBAS // BLK, BLK)
    return pl.pallas_call(
        half_kernel,
        grid=(PDEV // P_STEP,),
        in_specs=[
            pl.BlockSpec((NB, 2), lambda s: (0, 0)),
            pl.BlockSpec((NOCC, NBAS // BLK, BLK), lambda s: (0, 0, 0)),
        ]
        + [
            pl.BlockSpec((P_STEP // LOADS, NB, BLK * BLK), functools.partial(lambda n, s: (s * LOADS + n, 0, 0), n))
            for n in range(LOADS)
        ],
        out_specs=pl.BlockSpec((NOCC * PDEV, WIDE), lambda s: (0, 0)),
        out_shape=jax.ShapeDtypeStruct((NOCC * PDEV, WIDE), BF16),
        scratch_shapes=[
            pltpu.VMEM((NOCC, NB, BLK * BLK), F32),
            pltpu.VMEM((NOCC, PDEV, NCOMP), F32),
        ],
        compiler_params=params(16),
        cost_estimate=CHEAP,
        name="half",
    )(pairs, occ, *[integrals] * LOADS)


ANYWHERE = pl.BlockSpec(memory_space=pl.ANY)


def shaped(*shape, dtype=BF16):
    return jax.ShapeDtypeStruct(shape, dtype)


def cut_kernel(pos_ref, s_ref, o_ref, sems):
    copies = []
    for k in range(4):
        cols = pl.ds(pl.multiple_of((k * 2 + pos_ref[4]) * HCOL, 128), HCOL)
        copies.append(pltpu.make_async_copy(s_ref.at[:, cols], o_ref.at[k], sems.at[k]))
    for copy in copies:
        copy.start()
    for copy in copies:
        copy.wait()


def cut(pos, stored):
    return pl.pallas_call(
        cut_kernel,
        in_specs=[SMEM, pl.BlockSpec(memory_space=pltpu.HBM)],
        out_specs=VMEM,
        out_shape=shaped(4, 256, HCOL),
        scratch_shapes=[pltpu.SemaphoreType.DMA((4,))],
        compiler_params=params(60),
        cost_estimate=CHEAP,
        name="cut",
    )(pos, stored)


def hold_stored_kernel(pos_ref, *refs):
    sems = refs[4]
    zh, core = pos_ref[3], pos_ref[4]
    copies = []
    for h in range(2):
        for d in range(4):
            for o in range(2):
                start = lax.rem(zh - d + 4, 4) * 2 * PDEV + (1 - core if o else core) * PDEV
                src = refs[h].at[:, pl.ds(pl.multiple_of(start, PDEV), PDEV), :]
                dst = refs[2 + h].at[:, pl.ds((2 * d + o) * PDEV, PDEV), :]
                copies.append(pltpu.make_async_copy(src, dst, sems.at[h * 8 + 2 * d + o]))
    for copy in copies:
        copy.start()
    for copy in copies:
        copy.wait()


def hold_stored(pos, mine, other):
    return pl.pallas_call(
        hold_stored_kernel,
        in_specs=[SMEM] + [ANYWHERE] * 2,
        out_specs=[VMEM] * 2,
        out_shape=[shaped(4, 256, HCOL)] * 2,
        scratch_shapes=[pltpu.SemaphoreType.DMA((16,))],
        compiler_params=params(16),
        cost_estimate=CHEAP,
        name="hold_stored",
    )(pos, mine, other)


def factor_kernel(*refs):
    v_ref, out_ref, h_ref, pick_ref, f_ref, nu_ref, nus_ref, sems = refs[8:]
    loads = [pltpu.make_async_copy(refs[row], h_ref.at[row], sems.at[row]) for row in range(8)]
    for load in loads:
        load.start()
    for load in loads:
        load.wait()
    for row in range(8):
        nu_ref[row : row + 1] = h_ref[row, :, NCOMP:].astype(F32)[0:1].astype(jnp.int32)
    copy = pltpu.make_async_copy(nu_ref, nus_ref, sems.at[8])
    copy.start()
    copy.wait()
    for row in range(8):
        slot = row % 2
        for k in range(NB):
            n = nus_ref[row, k]
            pick_ref[slot, k * BLK : (k + 1) * BLK, :] = v_ref[pl.ds(pl.multiple_of(n * BLK, BLK), BLK), :]
        f = jnp.dot(h_ref[row, :, :NCOMP], pick_ref[slot], preferred_element_type=F32)
        for i in range(NOCC):
            f_ref[i, row * PDEV : (row + 1) * PDEV, :] = f[i * PDEV : (i + 1) * PDEV]
    for i in range(NOCC):
        turned = jnp.transpose(f_ref[i])
        rows = [turned[k * 96 + n * 12 : k * 96 + n * 12 + 12] for n in range(8) for k in range(4)]
        out_ref[i * SLAB : (i + 1) * SLAB, :] = jnp.concatenate(rows, axis=0).astype(BF16)


def factors(pieces, virtual):
    return pl.pallas_call(
        factor_kernel,
        in_specs=[ANYWHERE] * 8 + [VMEM],
        out_specs=VMEM,
        out_shape=shaped(NOCC * SLAB, KDIM),
        scratch_shapes=[
            pltpu.VMEM((8, NOCC * PDEV, WIDE), BF16),
            pltpu.VMEM((2, NCOMP, SLAB), BF16),
            pltpu.VMEM((NOCC, KDIM, SLAB), F32),
            pltpu.VMEM((8, 128), jnp.int32),
            pltpu.SMEM((8, 128), jnp.int32),
            pltpu.SemaphoreType.DMA((9,)),
        ],
        compiler_params=params(16),
        cost_estimate=CHEAP,
        name="factor",
    )(*pieces, virtual)


def panel_kernel(pos_ref, *refs):
    f, parts, out_ref, wide_ref, sems = refs[:4], refs[4:6], *refs[6:]
    loads = []
    for d in range(4):
        start = lax.rem(pos_ref[0] - d + 4, 4) * KDIM
        cols = pl.ds(pl.multiple_of(start, KDIM), KDIM)
        loads.append(pltpu.make_async_copy(f[d], wide_ref.at[:, cols], sems.at[d]))
    for load in loads:
        load.start()
    for load in loads:
        load.wait()
    for i in range(NOCC):
        for h in range(2):
            rows = parts[h][...].reshape(4 * 256, HCOL)
            value = jnp.dot(wide_ref[i * SLAB : (i + 1) * SLAB], rows, preferred_element_type=F32).astype(BF16)
            out_ref[:, i * 48 : i * 48 + 48, h * HCOL : (h + 1) * HCOL] = value.reshape(8, 48, HCOL)


def panel(pos, f, mine, other):
    return pl.pallas_call(
        panel_kernel,
        in_specs=[SMEM] + [ANYWHERE] * 4 + [VMEM] * 2,
        out_specs=VMEM,
        out_shape=shaped(8, NOCC * 48, NCOL),
        scratch_shapes=[
            pltpu.VMEM((NOCC * SLAB, 4 * 256), BF16),
            pltpu.SemaphoreType.DMA((4,)),
        ],
        compiler_params=params(20),
        cost_estimate=CHEAP,
        name="panel",
    )(pos, *f, mine, other)


def join_kernel(got_ref, out_ref):
    for i in range(NOCC):
        rows = slice(i * 48, i * 48 + 48)
        value = got_ref[0, rows, :].astype(F32)
        for n in range(1, 8):
            value = value + got_ref[n, rows, :].astype(F32)
        for k in range(4):
            out_ref[k, i * 12 : i * 12 + 12, :] = value[k * 12 : k * 12 + 12].astype(BF16)


def join(got):
    return pl.pallas_call(
        join_kernel,
        in_specs=[VMEM],
        out_specs=VMEM,
        out_shape=shaped(4, 24, NCOL),
        compiler_params=params(16),
        cost_estimate=CHEAP,
        name="join",
    )(got)


def place_kernel(pos_ref, a_ref, o_ref):
    core = pos_ref[4]
    for k in range(4):
        for h in range(2):
            half = 1 - core if h else core
            cols = pl.ds(pl.multiple_of(k * NCOL + half * HCOL, 128), HCOL)
            piece = slice(h * HCOL, (h + 1) * HCOL)
            for i in range(2):
                o_ref[i, :, cols] = a_ref[k, i * 12 : i * 12 + 12, piece]


GROUPS_X = [[x * 8 + r for x in range(4)] for r in range(8)]
GROUPS_YZ = [[x * 8 + r for r in range(8)] for x in range(4)]


def spread(value, groups):
    return lax.all_to_all(value, "aux", 0, 0, axis_index_groups=groups, tiled=True)


def per_device(integrals, block_pairs, occupied, virtual, stored):
    aux, grp = lax.axis_index("aux"), lax.axis_index("grp")
    x, y, zl = aux // 8, (aux // 2) % 4, aux % 2
    zh, core = grp // 2, grp % 2
    pos = jnp.stack([x, y, zl, zh, core]).astype(jnp.int32)

    half = half_transform(integrals, block_pairs[0], occupied)
    half, virtual, stored = lax.optimization_barrier((half, virtual, stored))
    got = spread(cut(pos, stored), GROUPS_X)
    pieces = []
    for d in range(4):
        pieces.append(lax.ppermute(half, "grp", shift_zh(d)) if d else half)
        pieces.append(lax.ppermute(pieces[-1], "grp", SWAP_CORE))
    f = factors(pieces, virtual)
    got, f = lax.optimization_barrier((got, f))
    near = [f] + [lax.ppermute(f, "aux", shift_x(d)) for d in (1, 2, 3)]
    other = lax.ppermute(got, "grp", SWAP_CORE)
    mine, other = hold_stored(pos, got, other)
    summed = join(spread(panel(pos, near, mine, other), GROUPS_YZ))
    out = pl.pallas_call(
        place_kernel,
        in_specs=[SMEM, VMEM],
        out_specs=VMEM,
        out_shape=shaped(2, 12, JWIN * V),
        compiler_params=params(16),
        cost_estimate=CHEAP,
        name="place",
    )(pos, spread(summed, GROUPS_X))
    return out.reshape(NOCC, 12, JWIN, V)


def solution(mesh):
    in_specs = (
        P(("aux", "grp"), None, None),
        P(("aux", "grp"), None, None),
        P(),
        P(None, "grp"),
        P("aux", None),
    )
    out_specs = P(None, ("grp", "aux"), None, None)
    return jax.shard_map(
        per_device, mesh=mesh, in_specs=in_specs, out_specs=out_specs, check_vma=False
    )
```

```python
import functools

import jax
import jax.numpy as jnp
from jax import lax
from jax.experimental import pallas as pl
from jax.experimental.pallas import tpu as pltpu
from jax.sharding import PartitionSpec as P

NBAS = 4096
BLK = 64
V = 3072
NOCC = 2
JWIN = 2
NB = 16
PDEV = 32
RING = 4
SLAB = 384
NCOL = 1536
HCOL = 768
ROWS = 24
NCOMP = NB * BLK
KDIM = 8 * PDEV

F32 = jnp.float32
BF16 = jnp.bfloat16
VMEM = pl.BlockSpec(memory_space=pltpu.VMEM)
SMEM = pl.BlockSpec(memory_space=pltpu.SMEM)


def params(mib):
    return pltpu.CompilerParams(vmem_limit_bytes=mib * 1024 * 1024)


CHEAP = pl.CostEstimate(flops=0, bytes_accessed=0, transcendentals=0)


def shift_x(d):
    return [(a, ((a // 8 + d) % 4) * 8 + a % 8) for a in range(32)]


SWAP_CORE = [(g, g ^ 1) for g in range(8)]


def shift_zh(d):
    return [(g, (g + 2 * d) % 8) for g in range(8)]


P_STEP = 8
WIDE = NCOMP + 128


LOADS = 4


def half_kernel(pairs_ref, occ_ref, *refs):
    xs = refs[:LOADS]
    o_ref, w_ref, sum_ref = refs[LOADS:]
    step = pl.program_id(0)

    @pl.when(step == 0)
    def _():
        pick = (pairs_ref[:, 0:1] == lax.broadcasted_iota(jnp.int32, (NB, BLK), 1)).astype(BF16)
        lane = lax.broadcasted_iota(jnp.int32, (BLK, BLK * BLK), 1)
        row = lax.broadcasted_iota(jnp.int32, (BLK, BLK * BLK), 0)
        spread = (lane // BLK == row).astype(BF16)
        for i in range(NOCC):
            rows = jnp.dot(pick, occ_ref[i], preferred_element_type=F32).astype(BF16)
            w_ref[i] = jnp.dot(rows, spread, preferred_element_type=F32)

    acc = [[jnp.zeros((NB, 128), F32) for _ in range(NOCC)] for _ in range(P_STEP)]
    for t in range(BLK * BLK // 128):
        cols = slice(t * 128, (t + 1) * 128)
        w = [w_ref[i, :, cols] for i in range(NOCC)]
        for p in range(P_STEP):
            x = xs[p * LOADS // P_STEP][p % (P_STEP // LOADS), :, cols].astype(F32)
            for i in range(NOCC):
                acc[p][i] = acc[p][i] + x * w[i]
    rows = P_STEP * NB
    lane = lax.broadcasted_iota(jnp.int32, (rows, NCOMP), 1)
    row = lax.broadcasted_iota(jnp.int32, (rows, NCOMP), 0)
    mine = lane // BLK == row % NB
    srow = lax.broadcasted_iota(jnp.int32, (P_STEP, rows), 0)
    scol = lax.broadcasted_iota(jnp.int32, (P_STEP, rows), 1)
    collect = (scol // NB == srow).astype(BF16)
    for i in range(NOCC):
        a = jnp.concatenate([acc[p][i] for p in range(P_STEP)], axis=0)
        both = a + pltpu.roll(a, BLK, 1)
        wide = jnp.concatenate([both] * (NCOMP // 128), axis=1)
        placed = jnp.where(mine, wide, 0.0).astype(BF16)
        at = pl.ds(pl.multiple_of(step * P_STEP, P_STEP), P_STEP)
        sum_ref[i, at, :] = jnp.dot(collect, placed, preferred_element_type=F32)

    @pl.when(step == PDEV // P_STEP - 1)
    def _():
        nrow = lax.broadcasted_iota(jnp.int32, (NB, 128), 0)
        ncol = lax.broadcasted_iota(jnp.int32, (NB, 128), 1)
        named = jnp.sum(jnp.where(nrow == ncol, pairs_ref[:, 1:2].astype(F32), 0.0), axis=0, keepdims=True)
        for i in range(NOCC):
            o_ref[i * PDEV : (i + 1) * PDEV, :NCOMP] = sum_ref[i].astype(BF16)
            o_ref[i * PDEV : (i + 1) * PDEV, NCOMP:] = jnp.broadcast_to(named, (PDEV, 128)).astype(BF16)


def half_transform(integrals, pairs, occupied):
    occ = occupied.reshape(NOCC, NBAS // BLK, BLK)
    return pl.pallas_call(
        half_kernel,
        grid=(PDEV // P_STEP,),
        in_specs=[
            pl.BlockSpec((NB, 2), lambda s: (0, 0)),
            pl.BlockSpec((NOCC, NBAS // BLK, BLK), lambda s: (0, 0, 0)),
        ]
        + [
            pl.BlockSpec((P_STEP // LOADS, NB, BLK * BLK), functools.partial(lambda n, s: (s * LOADS + n, 0, 0), n))
            for n in range(LOADS)
        ],
        out_specs=pl.BlockSpec((NOCC * PDEV, WIDE), lambda s: (0, 0)),
        out_shape=jax.ShapeDtypeStruct((NOCC * PDEV, WIDE), BF16),
        scratch_shapes=[
            pltpu.VMEM((NOCC, NB, BLK * BLK), F32),
            pltpu.VMEM((NOCC, PDEV, NCOMP), F32),
        ],
        compiler_params=params(16),
        cost_estimate=CHEAP,
        name="half",
    )(pairs, occ, *[integrals] * LOADS)


ANYWHERE = pl.BlockSpec(memory_space=pl.ANY)


def shaped(*shape, dtype=BF16):
    return jax.ShapeDtypeStruct(shape, dtype)


def cut_kernel(pos_ref, s_ref, o_ref, sems):
    copies = []
    for k in range(4):
        cols = pl.ds(pl.multiple_of((k * 2 + pos_ref[4]) * HCOL, 128), HCOL)
        copies.append(pltpu.make_async_copy(s_ref.at[:, cols], o_ref.at[k], sems.at[k]))
    for copy in copies:
        copy.start()
    for copy in copies:
        copy.wait()


def cut(pos, stored):
    return pl.pallas_call(
        cut_kernel,
        in_specs=[SMEM, pl.BlockSpec(memory_space=pltpu.HBM)],
        out_specs=VMEM,
        out_shape=shaped(4, 256, HCOL),
        scratch_shapes=[pltpu.SemaphoreType.DMA((4,))],
        compiler_params=params(60),
        cost_estimate=CHEAP,
        name="cut",
    )(pos, stored)


def hold_kernel(src, dst, sems):
    part = NBAS // LOADS
    copies = []
    for n in range(LOADS):
        rows = pl.ds(n * part, part)
        copies.append(pltpu.make_async_copy(src.at[rows], dst.at[rows], sems.at[n]))
    for copy in copies:
        copy.start()
    for copy in copies:
        copy.wait()


def hold_virtual(virtual):
    return pl.pallas_call(
        hold_kernel,
        in_specs=[ANYWHERE],
        out_specs=VMEM,
        out_shape=shaped(NBAS, SLAB),
        scratch_shapes=[pltpu.SemaphoreType.DMA((LOADS,))],
        compiler_params=params(16),
        cost_estimate=CHEAP,
        name="hold_virtual",
    )(virtual)


def hold_stored_kernel(pos_ref, *refs):
    sems = refs[4]
    zh, core = pos_ref[3], pos_ref[4]
    copies = []
    for h in range(2):
        for d in range(4):
            for o in range(2):
                start = lax.rem(zh - d + 4, 4) * 2 * PDEV + (1 - core if o else core) * PDEV
                src = refs[h].at[:, pl.ds(pl.multiple_of(start, PDEV), PDEV), :]
                dst = refs[2 + h].at[:, pl.ds((2 * d + o) * PDEV, PDEV), :]
                copies.append(pltpu.make_async_copy(src, dst, sems.at[h * 8 + 2 * d + o]))
    for copy in copies:
        copy.start()
    for copy in copies:
        copy.wait()


def hold_stored(pos, mine, other):
    return pl.pallas_call(
        hold_stored_kernel,
        in_specs=[SMEM] + [ANYWHERE] * 2,
        out_specs=[VMEM] * 2,
        out_shape=[shaped(4, 256, HCOL)] * 2,
        scratch_shapes=[pltpu.SemaphoreType.DMA((16,))],
        compiler_params=params(16),
        cost_estimate=CHEAP,
        name="hold_stored",
    )(pos, mine, other)


def factor_kernel(*refs):
    v_ref, out_ref, h_ref, pick_ref, f_ref, nu_ref, nus_ref, sems = refs[8:]
    loads = [pltpu.make_async_copy(refs[row], h_ref.at[row], sems.at[row]) for row in range(8)]
    for load in loads:
        load.start()
    for load in loads:
        load.wait()
    for row in range(8):
        nu_ref[row : row + 1] = h_ref[row, :, NCOMP:].astype(F32)[0:1].astype(jnp.int32)
    copy = pltpu.make_async_copy(nu_ref, nus_ref, sems.at[8])
    copy.start()
    copy.wait()
    for row in range(8):
        slot = row % 2
        for k in range(NB):
            n = nus_ref[row, k]
            pick_ref[slot, k * BLK : (k + 1) * BLK, :] = v_ref[pl.ds(pl.multiple_of(n * BLK, BLK), BLK), :]
        f = jnp.dot(h_ref[row, :, :NCOMP], pick_ref[slot], preferred_element_type=F32)
        for i in range(NOCC):
            f_ref[i, row * PDEV : (row + 1) * PDEV, :] = f[i * PDEV : (i + 1) * PDEV]
    for i in range(NOCC):
        turned = jnp.transpose(f_ref[i])
        rows = [turned[k * 96 + n * 12 : k * 96 + n * 12 + 12] for n in range(8) for k in range(4)]
        out_ref[i * SLAB : (i + 1) * SLAB, :] = jnp.concatenate(rows, axis=0).astype(BF16)


def factors(pieces, virtual):
    return pl.pallas_call(
        factor_kernel,
        in_specs=[ANYWHERE] * 8 + [VMEM],
        out_specs=VMEM,
        out_shape=shaped(NOCC * SLAB, KDIM),
        scratch_shapes=[
            pltpu.VMEM((8, NOCC * PDEV, WIDE), BF16),
            pltpu.VMEM((2, NCOMP, SLAB), BF16),
            pltpu.VMEM((NOCC, KDIM, SLAB), F32),
            pltpu.VMEM((8, 128), jnp.int32),
            pltpu.SMEM((8, 128), jnp.int32),
            pltpu.SemaphoreType.DMA((9,)),
        ],
        compiler_params=params(16),
        cost_estimate=CHEAP,
        name="factor",
    )(*pieces, virtual)


def panel_kernel(pos_ref, *refs):
    f, parts, out_ref, wide_ref, sems = refs[:4], refs[4:6], *refs[6:]
    loads = []
    for d in range(4):
        start = lax.rem(pos_ref[0] - d + 4, 4) * KDIM
        cols = pl.ds(pl.multiple_of(start, KDIM), KDIM)
        loads.append(pltpu.make_async_copy(f[d], wide_ref.at[:, cols], sems.at[d]))
    for load in loads:
        load.start()
    for load in loads:
        load.wait()
    for i in range(NOCC):
        for h in range(2):
            rows = parts[h][...].reshape(4 * 256, HCOL)
            value = jnp.dot(wide_ref[i * SLAB : (i + 1) * SLAB], rows, preferred_element_type=F32).astype(BF16)
            out_ref[:, i * 48 : i * 48 + 48, h * HCOL : (h + 1) * HCOL] = value.reshape(8, 48, HCOL)


def panel(pos, f, mine, other):
    return pl.pallas_call(
        panel_kernel,
        in_specs=[SMEM] + [ANYWHERE] * 4 + [VMEM] * 2,
        out_specs=VMEM,
        out_shape=shaped(8, NOCC * 48, NCOL),
        scratch_shapes=[
            pltpu.VMEM((NOCC * SLAB, 4 * 256), BF16),
            pltpu.SemaphoreType.DMA((4,)),
        ],
        compiler_params=params(20),
        cost_estimate=CHEAP,
        name="panel",
    )(pos, *f, mine, other)


def join_kernel(pos_ref, got_ref, *refs):
    outs, sum_ref = refs[:4], refs[4]
    for i in range(NOCC):
        rows = slice(i * 48, i * 48 + 48)
        value = got_ref[0, rows, :].astype(F32)
        for n in range(1, 8):
            value = value + got_ref[n, rows, :].astype(F32)
        for k in range(4):
            sum_ref[k, i * 12 : i * 12 + 12, :] = value[k * 12 : k * 12 + 12]
    for d in range(4):
        outs[d][...] = sum_ref[lax.rem(pos_ref[0] + d, 4)].astype(BF16)


def join(pos, got):
    return pl.pallas_call(
        join_kernel,
        in_specs=[SMEM, VMEM],
        out_specs=[VMEM] * 4,
        out_shape=[shaped(24, NCOL)] * 4,
        scratch_shapes=[pltpu.VMEM((4, 24, NCOL), F32)],
        compiler_params=params(16),
        cost_estimate=CHEAP,
        name="join",
    )(pos, got)


def place_kernel(pos_ref, *refs):
    o_ref = refs[4]
    core = pos_ref[4]
    for d in range(4):
        at = lax.rem(pos_ref[0] - d + 4, 4) * NCOL
        for h in range(2):
            half = 1 - core if h else core
            cols = pl.ds(pl.multiple_of(at + half * HCOL, 128), HCOL)
            piece = slice(h * HCOL, (h + 1) * HCOL)
            for i in range(2):
                o_ref[i, :, cols] = refs[d][i * 12 : i * 12 + 12, piece]


GROUPS_X = [[x * 8 + r for x in range(4)] for r in range(8)]
GROUPS_YZ = [[x * 8 + r for r in range(8)] for x in range(4)]


def spread(value, groups):
    return lax.all_to_all(value, "aux", 0, 0, axis_index_groups=groups, tiled=True)


def per_device(integrals, block_pairs, occupied, virtual, stored):
    aux, grp = lax.axis_index("aux"), lax.axis_index("grp")
    x, y, zl = aux // 8, (aux // 2) % 4, aux % 2
    zh, core = grp // 2, grp % 2
    pos = jnp.stack([x, y, zl, zh, core]).astype(jnp.int32)

    got = spread(cut(pos, stored), GROUPS_X)
    half = half_transform(integrals, block_pairs[0], occupied)
    swapped = lax.ppermute(half, "grp", SWAP_CORE)
    near = {d: lax.ppermute(half, "grp", shift_zh(d)) for d in (1, 2, 3)}
    near[1], virtual = lax.optimization_barrier((near[1], virtual))
    virtual = hold_virtual(virtual)
    near[1], virtual = lax.optimization_barrier((near[1], virtual))
    pieces = [half, swapped]
    for d in (1, 2, 3):
        pieces += [near[d], lax.ppermute(near[d], "grp", SWAP_CORE)]
    f = factors(pieces, virtual)
    got, f = lax.optimization_barrier((got, f))
    near = {d: lax.ppermute(f, "aux", shift_x(d)) for d in (2, 1, 3)}
    near = [f] + [near[d] for d in (1, 2, 3)]
    other = lax.ppermute(got, "grp", SWAP_CORE)
    mine, other = hold_stored(pos, got, other)
    ends = join(pos, spread(panel(pos, near, mine, other), GROUPS_YZ))
    out = pl.pallas_call(
        place_kernel,
        in_specs=[SMEM] + [VMEM] * 4,
        out_specs=VMEM,
        out_shape=shaped(NOCC, 12, JWIN * V),
        compiler_params=params(16),
        cost_estimate=CHEAP,
        name="place",
    )(pos, ends[0], *[lax.ppermute(ends[d], "aux", shift_x(d)) for d in (1, 2, 3)])
    return out.reshape(NOCC, 12, JWIN, V)

def solution(mesh):
    in_specs = (
        P(("aux", "grp"), None, None),
        P(("aux", "grp"), None, None),
        P(),
        P(None, "grp"),
        P("aux", None),
    )
    out_specs = P(None, ("grp", "aux"), None, None)
    return jax.shard_map(
        per_device, mesh=mesh, in_specs=in_specs, out_specs=out_specs, check_vma=False
    )
```

```python
import functools

import jax
import jax.numpy as jnp
from jax import lax
from jax.experimental import pallas as pl
from jax.experimental.pallas import tpu as pltpu
from jax.sharding import PartitionSpec as P

NBAS = 4096
BLK = 64
V = 3072
NOCC = 2
JWIN = 2
NB = 16
PDEV = 32
RING = 4
SLAB = 384
NCOL = 1536
HCOL = 768
ROWS = 24
NCOMP = NB * BLK
KDIM = 8 * PDEV

F32 = jnp.float32
BF16 = jnp.bfloat16
VMEM = pl.BlockSpec(memory_space=pltpu.VMEM)
SMEM = pl.BlockSpec(memory_space=pltpu.SMEM)


def params(mib):
    return pltpu.CompilerParams(vmem_limit_bytes=mib * 1024 * 1024)


CHEAP = pl.CostEstimate(flops=0, bytes_accessed=0, transcendentals=0)


def shift_x(d):
    return [(a, ((a // 8 + d) % 4) * 8 + a % 8) for a in range(32)]


SWAP_CORE = [(g, g ^ 1) for g in range(8)]


def shift_zh(d):
    return [(g, (g + 2 * d) % 8) for g in range(8)]


P_STEP = 8
WIDE = NCOMP + 128


LOADS = 4


def half_kernel(pairs_ref, occ_ref, *refs):
    xs = refs[:LOADS]
    o_ref, w_ref, sum_ref = refs[LOADS:]
    step = pl.program_id(0)

    @pl.when(step == 0)
    def _():
        pick = (pairs_ref[:, 0:1] == lax.broadcasted_iota(jnp.int32, (NB, BLK), 1)).astype(BF16)
        lane = lax.broadcasted_iota(jnp.int32, (BLK, BLK * BLK), 1)
        row = lax.broadcasted_iota(jnp.int32, (BLK, BLK * BLK), 0)
        spread = (lane // BLK == row).astype(BF16)
        for i in range(NOCC):
            rows = jnp.dot(pick, occ_ref[i], preferred_element_type=F32).astype(BF16)
            w_ref[i] = jnp.dot(rows, spread, preferred_element_type=F32)

    acc = [[jnp.zeros((NB, 128), F32) for _ in range(NOCC)] for _ in range(P_STEP)]
    for t in range(BLK * BLK // 128):
        cols = slice(t * 128, (t + 1) * 128)
        w = [w_ref[i, :, cols] for i in range(NOCC)]
        for p in range(P_STEP):
            x = xs[p * LOADS // P_STEP][p % (P_STEP // LOADS), :, cols].astype(F32)
            for i in range(NOCC):
                acc[p][i] = acc[p][i] + x * w[i]
    rows = P_STEP * NB
    lane = lax.broadcasted_iota(jnp.int32, (rows, NCOMP), 1)
    row = lax.broadcasted_iota(jnp.int32, (rows, NCOMP), 0)
    mine = lane // BLK == row % NB
    srow = lax.broadcasted_iota(jnp.int32, (P_STEP, rows), 0)
    scol = lax.broadcasted_iota(jnp.int32, (P_STEP, rows), 1)
    collect = (scol // NB == srow).astype(BF16)
    for i in range(NOCC):
        a = jnp.concatenate([acc[p][i] for p in range(P_STEP)], axis=0)
        both = a + pltpu.roll(a, BLK, 1)
        wide = jnp.concatenate([both] * (NCOMP // 128), axis=1)
        placed = jnp.where(mine, wide, 0.0).astype(BF16)
        at = pl.ds(pl.multiple_of(step * P_STEP, P_STEP), P_STEP)
        sum_ref[i, at, :] = jnp.dot(collect, placed, preferred_element_type=F32)

    @pl.when(step == PDEV // P_STEP - 1)
    def _():
        nrow = lax.broadcasted_iota(jnp.int32, (NB, 128), 0)
        ncol = lax.broadcasted_iota(jnp.int32, (NB, 128), 1)
        named = jnp.sum(jnp.where(nrow == ncol, pairs_ref[:, 1:2].astype(F32), 0.0), axis=0, keepdims=True)
        for i in range(NOCC):
            o_ref[i * PDEV : (i + 1) * PDEV, :NCOMP] = sum_ref[i].astype(BF16)
            o_ref[i * PDEV : (i + 1) * PDEV, NCOMP:] = jnp.broadcast_to(named, (PDEV, 128)).astype(BF16)


def half_transform(integrals, pairs, occupied):
    occ = occupied.reshape(NOCC, NBAS // BLK, BLK)
    return pl.pallas_call(
        half_kernel,
        grid=(PDEV // P_STEP,),
        in_specs=[
            pl.BlockSpec((NB, 2), lambda s: (0, 0)),
            pl.BlockSpec((NOCC, NBAS // BLK, BLK), lambda s: (0, 0, 0)),
        ]
        + [
            pl.BlockSpec((P_STEP // LOADS, NB, BLK * BLK), functools.partial(lambda n, s: (s * LOADS + n, 0, 0), n))
            for n in range(LOADS)
        ],
        out_specs=pl.BlockSpec((NOCC * PDEV, WIDE), lambda s: (0, 0)),
        out_shape=jax.ShapeDtypeStruct((NOCC * PDEV, WIDE), BF16),
        scratch_shapes=[
            pltpu.VMEM((NOCC, NB, BLK * BLK), F32),
            pltpu.VMEM((NOCC, PDEV, NCOMP), F32),
        ],
        compiler_params=params(16),
        cost_estimate=CHEAP,
        name="half",
    )(pairs, occ, *[integrals] * LOADS)


ANYWHERE = pl.BlockSpec(memory_space=pl.ANY)


def shaped(*shape, dtype=BF16):
    return jax.ShapeDtypeStruct(shape, dtype)


def cut_kernel(s_ref, o_ref, held_ref, sems):
    core = lax.rem(lax.axis_index("grp"), 2)
    reads, writes = [], []
    for k in range(4):
        cols = pl.ds(pl.multiple_of((k * 2 + core) * HCOL, 128), HCOL)
        reads.append(pltpu.make_async_copy(s_ref.at[:, cols], held_ref.at[k], sems.at[k]))
        writes.append(pltpu.make_async_copy(held_ref.at[k], o_ref.at[k], sems.at[4 + k]))
    for read in reads:
        read.start()
    for read, write in zip(reads, writes):
        read.wait()
        write.start()
    for write in writes:
        write.wait()


def cut(stored):
    return pl.pallas_call(
        cut_kernel,
        in_specs=[pl.BlockSpec(memory_space=pltpu.HBM)],
        out_specs=pl.BlockSpec(memory_space=pltpu.HBM),
        out_shape=shaped(4, 256, HCOL),
        scratch_shapes=[pltpu.VMEM((4, 256, HCOL), BF16), pltpu.SemaphoreType.DMA((8,))],
        compiler_params=params(60),
        cost_estimate=CHEAP,
        name="cut",
    )(stored)


def hold_kernel(src, dst, sems):
    part = NBAS // LOADS
    copies = []
    for n in range(LOADS):
        rows = pl.ds(n * part, part)
        copies.append(pltpu.make_async_copy(src.at[rows], dst.at[rows], sems.at[n]))
    for copy in copies:
        copy.start()
    for copy in copies:
        copy.wait()


def hold_virtual(virtual):
    return pl.pallas_call(
        hold_kernel,
        in_specs=[ANYWHERE],
        out_specs=VMEM,
        out_shape=shaped(NBAS, SLAB),
        scratch_shapes=[pltpu.SemaphoreType.DMA((LOADS,))],
        compiler_params=params(16),
        cost_estimate=CHEAP,
        name="hold_virtual",
    )(virtual)


def hold_stored_kernel(pos_ref, *refs):
    sems = refs[4]
    zh, core = pos_ref[3], pos_ref[4]
    copies = []
    for h in range(2):
        for d in range(4):
            for o in range(2):
                start = lax.rem(zh - d + 4, 4) * 2 * PDEV + (1 - core if o else core) * PDEV
                src = refs[h].at[:, pl.ds(pl.multiple_of(start, PDEV), PDEV), :]
                dst = refs[2 + h].at[:, pl.ds((2 * d + o) * PDEV, PDEV), :]
                copies.append(pltpu.make_async_copy(src, dst, sems.at[h * 8 + 2 * d + o]))
    for copy in copies:
        copy.start()
    for copy in copies:
        copy.wait()


def hold_stored(pos, mine, other):
    return pl.pallas_call(
        hold_stored_kernel,
        in_specs=[SMEM] + [ANYWHERE] * 2,
        out_specs=[VMEM] * 2,
        out_shape=[shaped(4, 256, HCOL)] * 2,
        scratch_shapes=[pltpu.SemaphoreType.DMA((16,))],
        compiler_params=params(16),
        cost_estimate=CHEAP,
        name="hold_stored",
    )(pos, mine, other)


def factor_kernel(*refs):
    v_ref, out_ref, h_ref, pick_ref, f_ref, nu_ref, nus_ref, sems = refs[8:]
    loads = [pltpu.make_async_copy(refs[row], h_ref.at[row], sems.at[row]) for row in range(8)]
    for load in loads:
        load.start()
    for load in loads:
        load.wait()
    for row in range(8):
        nu_ref[row : row + 1] = h_ref[row, :, NCOMP:].astype(F32)[0:1].astype(jnp.int32)
    copy = pltpu.make_async_copy(nu_ref, nus_ref, sems.at[8])
    copy.start()
    copy.wait()
    for row in range(8):
        slot = row % 2
        for k in range(NB):
            n = nus_ref[row, k]
            pick_ref[slot, k * BLK : (k + 1) * BLK, :] = v_ref[pl.ds(pl.multiple_of(n * BLK, BLK), BLK), :]
        f = jnp.dot(h_ref[row, :, :NCOMP], pick_ref[slot], preferred_element_type=F32)
        for i in range(NOCC):
            f_ref[i, row * PDEV : (row + 1) * PDEV, :] = f[i * PDEV : (i + 1) * PDEV]
    for i in range(NOCC):
        turned = jnp.transpose(f_ref[i])
        rows = [turned[k * 96 + n * 12 : k * 96 + n * 12 + 12] for n in range(8) for k in range(4)]
        out_ref[i * SLAB : (i + 1) * SLAB, :] = jnp.concatenate(rows, axis=0).astype(BF16)


def factors(pieces, virtual):
    return pl.pallas_call(
        factor_kernel,
        in_specs=[ANYWHERE] * 8 + [VMEM],
        out_specs=VMEM,
        out_shape=shaped(NOCC * SLAB, KDIM),
        scratch_shapes=[
            pltpu.VMEM((8, NOCC * PDEV, WIDE), BF16),
            pltpu.VMEM((2, NCOMP, SLAB), BF16),
            pltpu.VMEM((NOCC, KDIM, SLAB), F32),
            pltpu.VMEM((8, 128), jnp.int32),
            pltpu.SMEM((8, 128), jnp.int32),
            pltpu.SemaphoreType.DMA((9,)),
        ],
        compiler_params=params(16),
        cost_estimate=CHEAP,
        name="factor",
    )(*pieces, virtual)


def panel_kernel(pos_ref, *refs):
    f, parts, out_ref, wide_ref, sems = refs[:4], refs[4:6], *refs[6:]
    loads = []
    for d in range(4):
        start = lax.rem(pos_ref[0] - d + 4, 4) * KDIM
        cols = pl.ds(pl.multiple_of(start, KDIM), KDIM)
        loads.append(pltpu.make_async_copy(f[d], wide_ref.at[:, cols], sems.at[d]))
    for load in loads:
        load.start()
    for load in loads:
        load.wait()
    for i in range(NOCC):
        for h in range(2):
            rows = parts[h][...].reshape(4 * 256, HCOL)
            value = jnp.dot(wide_ref[i * SLAB : (i + 1) * SLAB], rows, preferred_element_type=F32).astype(BF16)
            out_ref[:, i * 48 : i * 48 + 48, h * HCOL : (h + 1) * HCOL] = value.reshape(8, 48, HCOL)


def panel(pos, f, mine, other):
    return pl.pallas_call(
        panel_kernel,
        in_specs=[SMEM] + [VMEM] * 6,
        out_specs=VMEM,
        out_shape=shaped(8, NOCC * 48, NCOL),
        scratch_shapes=[
            pltpu.VMEM((NOCC * SLAB, 4 * 256), BF16),
            pltpu.SemaphoreType.DMA((4,)),
        ],
        compiler_params=params(20),
        cost_estimate=CHEAP,
        name="panel",
    )(pos, *f, mine, other)


def join_kernel(pos_ref, got_ref, *refs):
    outs, sum_ref = refs[:4], refs[4]
    for i in range(NOCC):
        rows = slice(i * 48, i * 48 + 48)
        value = got_ref[0, rows, :].astype(F32)
        for n in range(1, 8):
            value = value + got_ref[n, rows, :].astype(F32)
        for k in range(4):
            sum_ref[k, i * 12 : i * 12 + 12, :] = value[k * 12 : k * 12 + 12]
    for d in range(4):
        outs[d][...] = sum_ref[lax.rem(pos_ref[0] + d, 4)].astype(BF16)


def join(pos, got):
    return pl.pallas_call(
        join_kernel,
        in_specs=[SMEM, VMEM],
        out_specs=[VMEM] * 4,
        out_shape=[shaped(24, NCOL)] * 4,
        scratch_shapes=[pltpu.VMEM((4, 24, NCOL), F32)],
        compiler_params=params(16),
        cost_estimate=CHEAP,
        name="join",
    )(pos, got)


def place_kernel(pos_ref, *refs):
    o_ref = refs[4]
    core = pos_ref[4]
    for d in range(4):
        at = lax.rem(pos_ref[0] - d + 4, 4) * NCOL
        for h in range(2):
            half = 1 - core if h else core
            cols = pl.ds(pl.multiple_of(at + half * HCOL, 128), HCOL)
            piece = slice(h * HCOL, (h + 1) * HCOL)
            for i in range(2):
                o_ref[i, :, cols] = refs[d][i * 12 : i * 12 + 12, piece]


GROUPS_X = [[x * 8 + r for x in range(4)] for r in range(8)]
GROUPS_YZ = [[x * 8 + r for r in range(8)] for x in range(4)]


def spread(value, groups):
    return lax.all_to_all(value, "aux", 0, 0, axis_index_groups=groups, tiled=True)


def per_device(integrals, block_pairs, occupied, virtual, stored):
    aux, grp = lax.axis_index("aux"), lax.axis_index("grp")
    x, y, zl = aux // 8, (aux // 2) % 4, aux % 2
    zh, core = grp // 2, grp % 2
    pos = jnp.stack([x, y, zl, zh, core]).astype(jnp.int32)

    got = spread(cut(stored), GROUPS_X)
    half = half_transform(integrals, block_pairs[0], occupied)
    swapped = lax.ppermute(half, "grp", SWAP_CORE)
    near = {d: lax.ppermute(half, "grp", shift_zh(d)) for d in (1, 2, 3)}
    near[1], virtual = lax.optimization_barrier((near[1], virtual))
    virtual = hold_virtual(virtual)
    near[1], virtual = lax.optimization_barrier((near[1], virtual))
    pieces = [half, swapped]
    for d in (1, 2, 3):
        pieces += [near[d], lax.ppermute(near[d], "grp", SWAP_CORE)]
    f = factors(pieces, virtual)
    got, f = lax.optimization_barrier((got, f))
    near = {d: lax.ppermute(f, "aux", shift_x(d)) for d in (2, 1, 3)}
    near = [f] + [near[d] for d in (1, 2, 3)]
    other = lax.ppermute(got, "grp", SWAP_CORE)
    mine, other = hold_stored(pos, got, other)
    ends = join(pos, spread(panel(pos, near, mine, other), GROUPS_YZ))
    out = pl.pallas_call(
        place_kernel,
        in_specs=[SMEM] + [VMEM] * 4,
        out_specs=VMEM,
        out_shape=shaped(NOCC, 12, JWIN * V),
        compiler_params=params(16),
        cost_estimate=CHEAP,
        name="place",
    )(pos, ends[0], *[lax.ppermute(ends[d], "aux", shift_x(d)) for d in (1, 2, 3)])
    return out.reshape(NOCC, 12, JWIN, V)

def solution(mesh):
    in_specs = (
        P(("aux", "grp"), None, None),
        P(("aux", "grp"), None, None),
        P(),
        P(None, "grp"),
        P("aux", None),
    )
    out_specs = P(None, ("grp", "aux"), None, None)
    return jax.shard_map(
        per_device, mesh=mesh, in_specs=in_specs, out_specs=out_specs, check_vma=False
    )
```

```python
import functools

import jax
import jax.numpy as jnp
from jax import lax
from jax.experimental import pallas as pl
from jax.experimental.pallas import tpu as pltpu
from jax.sharding import PartitionSpec as P

NBAS = 4096
BLK = 64
V = 3072
NOCC = 2
JWIN = 2
NB = 16
PDEV = 32
RING = 4
SLAB = 384
NCOL = 1536
HCOL = 768
ROWS = 24
NCOMP = NB * BLK
KDIM = 8 * PDEV

F32 = jnp.float32
BF16 = jnp.bfloat16
VMEM = pl.BlockSpec(memory_space=pltpu.VMEM)
SMEM = pl.BlockSpec(memory_space=pltpu.SMEM)


def params(mib):
    return pltpu.CompilerParams(vmem_limit_bytes=mib * 1024 * 1024)


CHEAP = pl.CostEstimate(flops=0, bytes_accessed=0, transcendentals=0)


def shift_x(d):
    return [(a, ((a // 8 + d) % 4) * 8 + a % 8) for a in range(32)]


SWAP_CORE = [(g, g ^ 1) for g in range(8)]


def shift_zh(d):
    return [(g, (g + 2 * d) % 8) for g in range(8)]


P_STEP = 8
WIDE = NCOMP + 128


LOADS = 4


def half_kernel(pairs_ref, occ_ref, *refs):
    xs = refs[:LOADS]
    o_ref, w_ref, sum_ref = refs[LOADS:]
    step = pl.program_id(0)

    @pl.when(step == 0)
    def _():
        pick = (pairs_ref[:, 0:1] == lax.broadcasted_iota(jnp.int32, (NB, BLK), 1)).astype(BF16)
        lane = lax.broadcasted_iota(jnp.int32, (BLK, BLK * BLK), 1)
        row = lax.broadcasted_iota(jnp.int32, (BLK, BLK * BLK), 0)
        spread = (lane // BLK == row).astype(BF16)
        for i in range(NOCC):
            rows = jnp.dot(pick, occ_ref[i], preferred_element_type=F32).astype(BF16)
            w_ref[i] = jnp.dot(rows, spread, preferred_element_type=F32)

    acc = [[jnp.zeros((NB, 128), F32) for _ in range(NOCC)] for _ in range(P_STEP)]
    for t in range(BLK * BLK // 128):
        cols = slice(t * 128, (t + 1) * 128)
        w = [w_ref[i, :, cols] for i in range(NOCC)]
        for p in range(P_STEP):
            x = xs[p * LOADS // P_STEP][p % (P_STEP // LOADS), :, cols].astype(F32)
            for i in range(NOCC):
                acc[p][i] = acc[p][i] + x * w[i]
    rows = P_STEP * NB
    lane = lax.broadcasted_iota(jnp.int32, (rows, NCOMP), 1)
    row = lax.broadcasted_iota(jnp.int32, (rows, NCOMP), 0)
    mine = lane // BLK == row % NB
    srow = lax.broadcasted_iota(jnp.int32, (P_STEP, rows), 0)
    scol = lax.broadcasted_iota(jnp.int32, (P_STEP, rows), 1)
    collect = (scol // NB == srow).astype(BF16)
    for i in range(NOCC):
        a = jnp.concatenate([acc[p][i] for p in range(P_STEP)], axis=0)
        both = a + pltpu.roll(a, BLK, 1)
        wide = jnp.concatenate([both] * (NCOMP // 128), axis=1)
        placed = jnp.where(mine, wide, 0.0).astype(BF16)
        at = pl.ds(pl.multiple_of(step * P_STEP, P_STEP), P_STEP)
        sum_ref[i, at, :] = jnp.dot(collect, placed, preferred_element_type=F32)

    @pl.when(step == PDEV // P_STEP - 1)
    def _():
        nrow = lax.broadcasted_iota(jnp.int32, (NB, 128), 0)
        ncol = lax.broadcasted_iota(jnp.int32, (NB, 128), 1)
        named = jnp.sum(jnp.where(nrow == ncol, pairs_ref[:, 1:2].astype(F32), 0.0), axis=0, keepdims=True)
        for i in range(NOCC):
            o_ref[i * PDEV : (i + 1) * PDEV, :NCOMP] = sum_ref[i].astype(BF16)
            o_ref[i * PDEV : (i + 1) * PDEV, NCOMP:] = jnp.broadcast_to(named, (PDEV, 128)).astype(BF16)


def half_transform(integrals, pairs, occupied):
    occ = occupied.reshape(NOCC, NBAS // BLK, BLK)
    return pl.pallas_call(
        half_kernel,
        grid=(PDEV // P_STEP,),
        in_specs=[
            pl.BlockSpec((NB, 2), lambda s: (0, 0)),
            pl.BlockSpec((NOCC, NBAS // BLK, BLK), lambda s: (0, 0, 0)),
        ]
        + [
            pl.BlockSpec((P_STEP // LOADS, NB, BLK * BLK), functools.partial(lambda n, s: (s * LOADS + n, 0, 0), n))
            for n in range(LOADS)
        ],
        out_specs=pl.BlockSpec((NOCC * PDEV, WIDE), lambda s: (0, 0)),
        out_shape=jax.ShapeDtypeStruct((NOCC * PDEV, WIDE), BF16),
        scratch_shapes=[
            pltpu.VMEM((NOCC, NB, BLK * BLK), F32),
            pltpu.VMEM((NOCC, PDEV, NCOMP), F32),
        ],
        compiler_params=params(16),
        cost_estimate=CHEAP,
        name="half",
    )(pairs, occ, *[integrals] * LOADS)


ANYWHERE = pl.BlockSpec(memory_space=pl.ANY)


def shaped(*shape, dtype=BF16):
    return jax.ShapeDtypeStruct(shape, dtype)


def cut_kernel(s_ref, o_ref, held_ref, sems):
    core = lax.rem(lax.axis_index("grp"), 2)
    reads, writes = [], []
    for k in range(4):
        cols = pl.ds(pl.multiple_of((k * 2 + core) * HCOL, 128), HCOL)
        reads.append(pltpu.make_async_copy(s_ref.at[:, cols], held_ref.at[k], sems.at[k]))
        writes.append(pltpu.make_async_copy(held_ref.at[k], o_ref.at[k], sems.at[4 + k]))
    for read in reads:
        read.start()
    for read, write in zip(reads, writes):
        read.wait()
        write.start()
    for write in writes:
        write.wait()


def cut(stored):
    return pl.pallas_call(
        cut_kernel,
        in_specs=[pl.BlockSpec(memory_space=pltpu.HBM)],
        out_specs=pl.BlockSpec(memory_space=pltpu.HBM),
        out_shape=shaped(4, 256, HCOL),
        scratch_shapes=[pltpu.VMEM((4, 256, HCOL), BF16), pltpu.SemaphoreType.DMA((8,))],
        compiler_params=params(60),
        cost_estimate=CHEAP,
        name="cut",
    )(stored)


def hold_kernel(src, dst, sems):
    part = NBAS // LOADS
    copies = []
    for n in range(LOADS):
        rows = pl.ds(n * part, part)
        copies.append(pltpu.make_async_copy(src.at[rows], dst.at[rows], sems.at[n]))
    for copy in copies:
        copy.start()
    for copy in copies:
        copy.wait()


def hold_virtual(virtual):
    return pl.pallas_call(
        hold_kernel,
        in_specs=[ANYWHERE],
        out_specs=VMEM,
        out_shape=shaped(NBAS, SLAB),
        scratch_shapes=[pltpu.SemaphoreType.DMA((LOADS,))],
        compiler_params=params(16),
        cost_estimate=CHEAP,
        name="hold_virtual",
    )(virtual)


def hold_stored_kernel(pos_ref, *refs):
    sems = refs[4]
    zh, core = pos_ref[3], pos_ref[4]
    copies = []
    for h in range(2):
        for d in range(4):
            for o in range(2):
                start = lax.rem(zh - d + 4, 4) * 2 * PDEV + (1 - core if o else core) * PDEV
                src = refs[h].at[:, pl.ds(pl.multiple_of(start, PDEV), PDEV), :]
                dst = refs[2 + h].at[:, pl.ds((2 * d + o) * PDEV, PDEV), :]
                copies.append(pltpu.make_async_copy(src, dst, sems.at[h * 8 + 2 * d + o]))
    for copy in copies:
        copy.start()
    for copy in copies:
        copy.wait()


def hold_stored(pos, mine, other):
    return pl.pallas_call(
        hold_stored_kernel,
        in_specs=[SMEM] + [ANYWHERE] * 2,
        out_specs=[VMEM] * 2,
        out_shape=[shaped(4, 256, HCOL)] * 2,
        scratch_shapes=[pltpu.SemaphoreType.DMA((16,))],
        compiler_params=params(16),
        cost_estimate=CHEAP,
        name="hold_stored",
    )(pos, mine, other)


def factor_kernel(*refs):
    v_ref, out_ref, h_ref, pick_ref, f_ref, nu_ref, nus_ref, sems = refs[8:]
    loads = [pltpu.make_async_copy(refs[row], h_ref.at[row], sems.at[row]) for row in range(8)]
    for load in loads:
        load.start()
    for load in loads:
        load.wait()
    for row in range(8):
        nu_ref[row : row + 1] = h_ref[row, :, NCOMP:].astype(F32)[0:1].astype(jnp.int32)
    copy = pltpu.make_async_copy(nu_ref, nus_ref, sems.at[8])
    copy.start()
    copy.wait()
    for row in range(8):
        slot = row % 2
        for k in range(NB):
            n = nus_ref[row, k]
            pick_ref[slot, k * BLK : (k + 1) * BLK, :] = v_ref[pl.ds(pl.multiple_of(n * BLK, BLK), BLK), :]
        f = jnp.dot(h_ref[row, :, :NCOMP], pick_ref[slot], preferred_element_type=F32)
        for i in range(NOCC):
            f_ref[i, row * PDEV : (row + 1) * PDEV, :] = f[i * PDEV : (i + 1) * PDEV]
    for i in range(NOCC):
        turned = jnp.transpose(f_ref[i])
        rows = [turned[k * 96 + n * 12 : k * 96 + n * 12 + 12] for n in range(8) for k in range(4)]
        out_ref[i * SLAB : (i + 1) * SLAB, :] = jnp.concatenate(rows, axis=0).astype(BF16)


def factors(pieces, virtual):
    return pl.pallas_call(
        factor_kernel,
        in_specs=[ANYWHERE] * 8 + [VMEM],
        out_specs=VMEM,
        out_shape=shaped(NOCC * SLAB, KDIM),
        scratch_shapes=[
            pltpu.VMEM((8, NOCC * PDEV, WIDE), BF16),
            pltpu.VMEM((2, NCOMP, SLAB), BF16),
            pltpu.VMEM((NOCC, KDIM, SLAB), F32),
            pltpu.VMEM((8, 128), jnp.int32),
            pltpu.SMEM((8, 128), jnp.int32),
            pltpu.SemaphoreType.DMA((9,)),
        ],
        compiler_params=params(16),
        cost_estimate=CHEAP,
        name="factor",
    )(*pieces, virtual)


def panel_kernel(pos_ref, *refs):
    f, parts, out_ref, wide_ref, sems = refs[:4], refs[4:6], *refs[6:]
    loads = []
    for d in range(4):
        start = lax.rem(pos_ref[0] - d + 4, 4) * KDIM
        cols = pl.ds(pl.multiple_of(start, KDIM), KDIM)
        loads.append(pltpu.make_async_copy(f[d], wide_ref.at[:, cols], sems.at[d]))
    for load in loads:
        load.start()
    for load in loads:
        load.wait()
    for i in range(NOCC):
        for h in range(2):
            rows = parts[h][...].reshape(4 * 256, HCOL)
            value = jnp.dot(wide_ref[i * SLAB : (i + 1) * SLAB], rows, preferred_element_type=F32).astype(BF16)
            out_ref[:, i * 48 : i * 48 + 48, h * HCOL : (h + 1) * HCOL] = value.reshape(8, 48, HCOL)


def panel(pos, f, mine, other):
    return pl.pallas_call(
        panel_kernel,
        in_specs=[SMEM] + [VMEM] * 6,
        out_specs=VMEM,
        out_shape=shaped(8, NOCC * 48, NCOL),
        scratch_shapes=[
            pltpu.VMEM((NOCC * SLAB, 4 * 256), BF16),
            pltpu.SemaphoreType.DMA((4,)),
        ],
        compiler_params=params(20),
        cost_estimate=CHEAP,
        name="panel",
    )(pos, *f, mine, other)


def join_kernel(pos_ref, got_ref, *refs):
    outs, sum_ref = refs[:4], refs[4]
    for i in range(NOCC):
        rows = slice(i * 48, i * 48 + 48)
        value = got_ref[0, rows, :].astype(F32)
        for n in range(1, 8):
            value = value + got_ref[n, rows, :].astype(F32)
        for k in range(4):
            sum_ref[k, i] = value[k * 12 : k * 12 + 12]
    for d in range(4):
        outs[d][...] = sum_ref[lax.rem(pos_ref[0] + d, 4)].astype(BF16)


def join(pos, got):
    return pl.pallas_call(
        join_kernel,
        in_specs=[SMEM, VMEM],
        out_specs=[VMEM] * 4,
        out_shape=[shaped(NOCC, 12, NCOL)] * 4,
        scratch_shapes=[pltpu.VMEM((4, NOCC, 12, NCOL), F32)],
        compiler_params=params(16),
        cost_estimate=CHEAP,
        name="join",
    )(pos, got)


def place_kernel(pos_ref, *refs):
    o_ref = refs[4]
    core = pos_ref[4]
    for d in range(4):
        at = lax.rem(pos_ref[0] - d + 4, 4) * NCOL
        for h in range(2):
            half = 1 - core if h else core
            cols = pl.ds(pl.multiple_of(at + half * HCOL, 128), HCOL)
            piece = slice(h * HCOL, (h + 1) * HCOL)
            for i in range(2):
                o_ref[i, :, cols] = refs[d][i, :, piece]


GROUPS_X = [[x * 8 + r for x in range(4)] for r in range(8)]
GROUPS_YZ = [[x * 8 + r for r in range(8)] for x in range(4)]


def spread(value, groups):
    return lax.all_to_all(value, "aux", 0, 0, axis_index_groups=groups, tiled=True)


def per_device(integrals, block_pairs, occupied, virtual, stored):
    aux, grp = lax.axis_index("aux"), lax.axis_index("grp")
    x, y, zl = aux // 8, (aux // 2) % 4, aux % 2
    zh, core = grp // 2, grp % 2
    pos = jnp.stack([x, y, zl, zh, core]).astype(jnp.int32)

    got = spread(cut(stored), GROUPS_X)
    half = half_transform(integrals, block_pairs[0], occupied)
    swapped = lax.ppermute(half, "grp", SWAP_CORE)
    near = {d: lax.ppermute(half, "grp", shift_zh(d)) for d in (1, 2, 3)}
    near[1], virtual = lax.optimization_barrier((near[1], virtual))
    virtual = hold_virtual(virtual)
    near[1], virtual = lax.optimization_barrier((near[1], virtual))
    pieces = [half, swapped]
    for d in (1, 2, 3):
        pieces += [near[d], lax.ppermute(near[d], "grp", SWAP_CORE)]
    f = factors(pieces, virtual)
    got, f = lax.optimization_barrier((got, f))
    near = {d: lax.ppermute(f, "aux", shift_x(d)) for d in (2, 1, 3)}
    near = [f] + [near[d] for d in (1, 2, 3)]
    other = lax.ppermute(got, "grp", SWAP_CORE)
    mine, other = hold_stored(pos, got, other)
    ends = join(pos, spread(panel(pos, near, mine, other), GROUPS_YZ))
    out = pl.pallas_call(
        place_kernel,
        in_specs=[SMEM] + [VMEM] * 4,
        out_specs=VMEM,
        out_shape=shaped(NOCC, 12, JWIN * V),
        compiler_params=params(16),
        cost_estimate=CHEAP,
        name="place",
    )(pos, ends[0], *[lax.ppermute(ends[d], "aux", shift_x(d)) for d in (1, 2, 3)])
    return out.reshape(NOCC, 12, JWIN, V)

def solution(mesh):
    in_specs = (
        P(("aux", "grp"), None, None),
        P(("aux", "grp"), None, None),
        P(),
        P(None, "grp"),
        P("aux", None),
    )
    out_specs = P(None, ("grp", "aux"), None, None)
    return jax.shard_map(
        per_device, mesh=mesh, in_specs=in_specs, out_specs=out_specs, check_vma=False
    )
```
